32 devices in a mesh: dp: 4 (over y, x), vocab: 8 (over z, core).
Axes of the slice: x: 2, y: 2, z: 4, core: 2. Of those that a mesh axis runs over, the one named last changes fastest.
Arguments:
- features: bfloat16 [2048, 4096], P(('dp', 'vocab')), may hold values from -8 to 8
- head: bfloat16 [8192, 4096], P(('dp', 'vocab')), may hold values from -0.5 to 0.5
- momentum: bfloat16 [8192, 4096], P(('dp', 'vocab')), may hold values from -4.5597553e-06 to 4.5597553e-06
- hessian: bfloat16 [8192, 4096], P(('dp', 'vocab')), may hold values from 3.0500814e-08 to 0.00030517578
- true_labels: int32 [2048], replicated, may hold values from 0 to 8191
- sampled_labels: int32 [2048], replicated, may hold values from 0 to 8191
Outputs:
- mean_loss: float32 [], replicated
- new_hessian: bfloat16 [8192, 4096], P(('dp', 'vocab'))
- update: bfloat16 [8192, 4096], P(('dp', 'vocab'))
The draws below stay inside these ranges and needn't reach their ends.
All inputs are finite; a program needn't handle non-finite values.
Results may differ from the reference program's by a relative error of at most 0.019.
Values may be sent and summed in bfloat16 or wider, within the bound.
No kernel may reach another device: no remote copies, remote signals or barrier semaphores. Data moves between devices by JAX's collectives and lax.ppermute only.
A program may use at most 128 MiB of HBM per device.

```python
import math
import jax
import jax.numpy as jnp
import numpy as np
from jax import lax

D = 4096
TOK_DEV = 512
TOKENS = 2048
VOCAB = 8192
N_DP = 4


def head_rows(key, wanted):
    row_key = jax.random.fold_in(key, 11)

    def single(index):
        return jax.random.normal(jax.random.fold_in(row_key, index), (D,), jnp.float32)
    return jax.vmap(single)(wanted) * (3.0 / math.sqrt(D))


def draw_head(key, part):
    every_row = head_rows(key, jnp.arange(VOCAB, dtype=jnp.int32))
    return jnp.clip(every_row, -0.5, 0.5).astype(jnp.bfloat16)


def draw_features(key, part):
    own_key = jax.random.fold_in(key, 5)
    values = jax.random.normal(own_key, (TOKENS, D), jnp.float32)
    return jnp.clip(values, -8.0, 8.0).astype(jnp.bfloat16)


def set_ends(drawn, stream_key, low, largest):
    longest = drawn.shape.index(max(drawn.shape))
    spots = []
    for shift in (0, 1):
        where = [jax.random.randint(jax.random.fold_in(stream_key, axis), (), 0, length) for axis, length in enumerate(drawn.shape)]
        where[longest] = (where[longest] + shift) % drawn.shape[longest]
        spots.append(tuple(where))
    return drawn.at[spots[0]].set(low).at[spots[1]].set(largest)


def level_of(rng, shape, shards, least, largest):
    def one(position, parts):
        draws = jax.random.uniform(jax.random.fold_in(jax.random.fold_in(rng, 6), position), (parts,), jnp.float32, least / len(shards), largest / len(shards))
        return jnp.repeat(jnp.exp(draws), shape[position] // parts).reshape((-1,) + (1,) * (len(shape) - position - 1))

    loudness = one(*shards[0])
    for cut in shards[1:]:
        loudness = loudness * one(*cut)
    return loudness


def cumulative_ranks(number_of, lean):
    portions = [(1 << 20) // math.isqrt(grade ** lean) + 1 for grade in range(1, number_of + 1)]
    scale = 1 + sum(portions) // (1 << 30)
    return np.cumsum(np.array([max(1, weight // scale) for weight in portions]))


def skewed_ids(rng, extent, count, skew):
    grid = cumulative_ranks(count, skew)
    ticket = jax.random.randint(jax.random.fold_in(rng, 1), extent, 0, int(grid[count - 1]))
    grade = jnp.searchsorted(jnp.asarray(grid, jnp.int32), ticket, side="right")
    return jax.random.permutation(jax.random.fold_in(rng, 2), count)[grade].astype(jnp.int32)


def centred(stream_key, extent, spread, limit, shards=(), held_as=jnp.bfloat16):
    entries = jax.random.normal(stream_key, extent, jnp.float32) * spread
    if len(shards) > 0:
        entries = level_of(stream_key, extent, shards, -0.22, 0.18) * entries
    return jnp.clip(entries, min=-limit, max=limit).astype(held_as)


def setup_inputs(seed: int = 0) -> dict:
    key_of = jax.random.split(jax.random.key(seed), 7)
    features = draw_features(jax.random.fold_in(key_of[6], 71), 0)
    head = draw_head(jax.random.fold_in(key_of[6], 71), 0)
    momentum = centred(key_of[2], (VOCAB, D), (0.025 * TOKENS * VOCAB ** -2), 4.559755325317383e-06, ((0, 32),))
    hessian = jnp.clip(jnp.exp(math.log(0.00030517578) - 9.21089 * jax.random.uniform(key_of[3], (VOCAB, D), jnp.float32) ** level_of(key_of[3], (VOCAB, D), ((0, 32),), -0.2, 0.2)), 3.050081431865692e-08, 0.00030517578).astype(jnp.bfloat16)
    true_labels = set_ends(skewed_ids(key_of[4], (TOKENS,), VOCAB, 2), jax.random.fold_in(key_of[4], 3), 0, VOCAB - 1).astype(jnp.int32)
    sampled_labels = set_ends(skewed_ids(key_of[5], (TOKENS,), VOCAB, 1), jax.random.fold_in(key_of[5], 3), 0, VOCAB - 1).astype(jnp.int32)
    return dict(features=features, head=head, momentum=momentum, hessian=hessian, true_labels=true_labels, sampled_labels=sampled_labels)


hess_decay = 0.99
clip_scale = 0.05


def reference(features, head, momentum, hessian, true_labels, sampled_labels):
    logits = lax.dot_general(features, head, (((1,), (1,)), ((), ())), preferred_element_type=jnp.float32)
    log_norm = jax.nn.logsumexp(logits, axis=1)
    picked = jnp.take_along_axis(logits, true_labels[:, None].astype(jnp.int32), axis=1)[:, 0]
    mean_loss = jnp.mean(log_norm - picked)
    columns = jnp.arange(VOCAB, dtype=jnp.int32)
    chosen = (columns[None, :] == sampled_labels[:, None]).astype(jnp.float32)
    signal = (jnp.exp(logits - log_norm[:, None]) - chosen).astype(jnp.bfloat16)

    def add_group(total, index):
        start = (index * TOK_DEV).astype(jnp.int32)
        rows = lax.dynamic_slice_in_dim(signal, start, TOK_DEV, 0)
        group_rows = lax.dynamic_slice_in_dim(features, start, TOK_DEV, 0)
        partial_sum = lax.dot_general(rows, group_rows, (((0,), (0,)), ((), ())), preferred_element_type=jnp.float32)
        rounded = lax.optimization_barrier(partial_sum.astype(jnp.bfloat16)).astype(jnp.float32)
        return total + rounded, None

    gradient, _ = lax.scan(add_group, jnp.zeros((VOCAB, D), jnp.float32), jnp.arange(N_DP, dtype=jnp.int32))
    fresh = hess_decay * hessian.astype(jnp.float32) + (1.0 - hess_decay) * gradient * gradient
    clipped = jnp.clip(momentum.astype(jnp.float32) / (clip_scale * fresh), -1.0, 1.0)
    return mean_loss, fresh.astype(jnp.bfloat16), clipped.astype(jnp.bfloat16)
```

```python
import functools

import jax
import jax.numpy as jnp
from jax import lax
from jax.experimental import pallas as pl
from jax.experimental.pallas import tpu as pltpu
from jax.sharding import Mesh, PartitionSpec as P

hess_decay = 0.99
clip_scale = 0.05
N_BLOCKS = 4
PARTS = 2
K_TILE = 2048
LANES = 2
OWNER = 4
OWN = OWNER + N_BLOCKS
C_TILE = 2048
T_TILE = 256
VMEM = 24 * 2**20


def from_all(value, axis, size):
    if size > N_BLOCKS:
        return list(lax.all_gather(value, axis))
    others = [lax.ppermute(value, axis, [(i, (i + s) % size) for i in range(size)]) for s in range(1, size)]
    return [value] + others


whole = pl.BlockSpec(memory_space=pltpu.VMEM)
scalars = pl.BlockSpec(memory_space=pltpu.SMEM)
anywhere = pl.BlockSpec(memory_space=pl.ANY)


def assemble_kernel(plan, *refs):
    outs = refs[-len(plan) :]
    for out, parts in zip(outs, plan):
        at = 0
        for index, begin, size in parts:
            out[at : at + size] = refs[index][begin : begin + size]
            at += size


def assemble(wanted, after=()):
    arrays, plan = [], []
    for parts in wanted:
        plan.append([])
        for array, begin, size in parts:
            places = [i for i, known in enumerate(arrays) if known is array]
            if not places:
                arrays.append(array)
            plan[-1].append((places[0] if places else len(arrays) - 1, begin, size))
    shapes = [(sum(part[2] for part in parts), arrays[0].shape[1]) for parts in plan]
    return pl.pallas_call(
        functools.partial(assemble_kernel, plan),
        in_specs=[whole] * len(arrays) + [anywhere] * len(after),
        out_specs=[whole] * len(shapes),
        out_shape=[jax.ShapeDtypeStruct(shape, jnp.bfloat16) for shape in shapes],
        compiler_params=pltpu.CompilerParams(vmem_limit_bytes=VMEM),
        cost_estimate=pl.CostEstimate(
            flops=0, bytes_accessed=4 * sum(r * w for r, w in shapes), transcendentals=0
        ),
    )(*arrays, *after)


def prepare_kernel(voc_dev, true, sampled, place, *ordered):
    dp, z, core = lax.axis_index("dp"), lax.axis_index("z"), lax.axis_index("core")
    for mask in range(OWNER):
        place[mask] = dp ^ mask
    for k in range(N_BLOCKS):
        place[OWNER + k] = lax.rem(z - k + N_BLOCKS, N_BLOCKS)
    base = (dp * N_BLOCKS + z) * 2
    place[OWN] = (base + core) * voc_dev
    place[OWN + 1] = (base + 1 - core) * voc_dev
    n_dp, chunks = OWNER, 2 * LANES
    width = true.shape[1]
    owner = lax.broadcasted_iota(jnp.int32, (N_BLOCKS, width), 1) // (width // n_dp)
    for labels, out in zip((true, sampled), ordered):
        turned = [pltpu.roll(labels[...], i * (width // chunks), 1) if i else labels[...] for i in range(chunks)]
        for lane in range(LANES):
            found = jnp.zeros((N_BLOCKS, width), jnp.int32)
            for d in range(n_dp):
                rows = slice(d * N_BLOCKS, (d + 1) * N_BLOCKS)
                by_core = [turned[(d - c * LANES - lane) % chunks][rows] for c in range(2)]
                found = jnp.where(owner == d, jnp.where(core == 0, *by_core), found)
            for b in range(N_BLOCKS):
                out[b, lane] = found[b : b + 1]


def prepare(true, sampled, voc_dev):
    tokens = true.shape[0] // 2 // N_BLOCKS // LANES
    return pl.pallas_call(
        functools.partial(prepare_kernel, voc_dev),
        in_specs=[whole] * 2,
        out_specs=[scalars, whole, whole],
        out_shape=[jax.ShapeDtypeStruct((OWN + 2,), jnp.int32)]
        + [jax.ShapeDtypeStruct((N_BLOCKS, LANES, 1, tokens), jnp.int32)] * 2,
        compiler_params=pltpu.CompilerParams(vmem_limit_bytes=VMEM),
        cost_estimate=pl.CostEstimate(flops=0, bytes_accessed=0, transcendentals=0),
    )(true.reshape(-1, tokens), sampled.reshape(-1, tokens))


def logits_kernel(groups, count, place, true, *rest):
    arrays, (head, head_other) = rest[:count], rest[count : count + 2]
    *table, rows, logits, stats, tops = rest[count + 2 :]
    voc, width = head.shape
    tokens = rows.shape[0] // len(groups)
    for number, (_, _, pieces) in enumerate(groups):
        for index, size, begin, slot, offset in pieces:
            start = number * tokens + offset
            if slot is not None:
                start = pl.multiple_of(start + place[slot] * (tokens // 4), 16)
            rows[pl.ds(start, size), :] = arrays[index][begin : begin + size]
    tile = min(K_TILE, width)
    for start in range(0, width, tile):
        columns = slice(start, start + tile)
        both = jnp.concatenate([head[:, columns], head_other[:, columns]], axis=0)
        found = lax.dot_general(
            both, rows[:, columns], (((1,), (1,)), ((), ())), preferred_element_type=jnp.float32
        )
        if start == 0:
            logits[...] = found
        else:
            logits[...] += found
    stats[...] = table[0][...] if table else jnp.zeros_like(stats)
    ids = lax.broadcasted_iota(jnp.int32, (voc, tokens), 0)
    for number, (block, lane, _) in enumerate(groups):
        values = logits[:, number * tokens : (number + 1) * tokens]
        highest = jnp.max(values, axis=0, keepdims=True)
        raised = jnp.exp(values - highest)
        total = jnp.sum(raised, axis=0, keepdims=True)
        owner = place[OWNER + block]
        labels = true[owner, lane]
        picked = jnp.where(ids + place[OWN] == labels, values[:voc], 0.0)
        picked += jnp.where(ids + place[OWN + 1] == labels, values[voc:], 0.0)
        stats[owner, lane, 0:1] = highest + jnp.log(total)
        stats[owner, lane, 1:2] = jnp.sum(picked, axis=0, keepdims=True)
        logits[:, number * tokens : (number + 1) * tokens] = raised
        tops[number] = highest


def block_logits(place, true, groups, head, head_other, stats):
    voc, width = head.shape
    tokens = true.shape[3]
    arrays, plan = [], []
    for block, lane, pieces in groups:
        plan.append((block, lane, []))
        for array, *where in pieces:
            known = [i for i, a in enumerate(arrays) if a is array]
            if not known:
                arrays.append(array)
            plan[-1][2].append((known[0] if known else len(arrays) - 1, *where))
    total = len(groups) * tokens
    return pl.pallas_call(
        functools.partial(logits_kernel, plan, len(arrays)),
        in_specs=[scalars] + [whole] * (len(arrays) + 3 + len(stats)),
        out_specs=[whole] * 4,
        out_shape=[
            jax.ShapeDtypeStruct((total, width), jnp.bfloat16),
            jax.ShapeDtypeStruct((2 * voc, total), jnp.float32),
            jax.ShapeDtypeStruct((*true.shape[:2], 2, tokens), jnp.float32),
            jax.ShapeDtypeStruct((len(groups), 1, tokens), jnp.float32),
        ],
        compiler_params=pltpu.CompilerParams(vmem_limit_bytes=VMEM),
        cost_estimate=pl.CostEstimate(
            flops=4 * voc * total * width,
            bytes_accessed=4 * (voc + total) * width,
            transcendentals=2 * voc * total,
        ),
    )(place, true, *arrays, head, head_other, *stats)


def fill_signal(order, place, log_norm, sampled, raised, tops, signal):
    tokens = sampled.shape[3]
    voc = signal.shape[0] // 2
    ids = lax.broadcasted_iota(jnp.int32, (voc, tokens), 0)
    for number, (block, lane) in enumerate(order):
        values = raised[number // LANES]
        here = (number % LANES) * tokens
        owner = place[OWNER + block]
        scale = jnp.exp(tops[number // LANES][number % LANES] - log_norm[owner, lane])
        for i in range(2):
            half = slice(i * voc, (i + 1) * voc)
            chosen = (ids + place[OWN + i] == sampled[owner, lane]).astype(jnp.float32)
            found = values[half, here : here + tokens] * scale - chosen
            signal[half, number * tokens : (number + 1) * tokens] = found.astype(jnp.bfloat16)


def combine(tables):
    norms = [table[:, :, 0:1] for table in tables]
    top = functools.reduce(jnp.maximum, norms)
    return top + jnp.log(sum(jnp.exp(norm - top) for norm in norms)), sum(table[:, :, 1:2] for table in tables)


def combine_kernel(*refs):
    *tables, out = refs
    out[:, :, 0:1], out[:, :, 1:2] = combine(tables)


def combine_call(tables):
    return pl.pallas_call(
        combine_kernel,
        out_shape=jax.ShapeDtypeStruct(tables[0].shape, jnp.float32),
        compiler_params=pltpu.CompilerParams(vmem_limit_bytes=VMEM),
        cost_estimate=pl.CostEstimate(flops=0, bytes_accessed=0, transcendentals=0),
    )(*tables)


def gradient_kernel(part, order, place, *refs):
    if part:
        signal, *rows, keep, send = refs
    else:
        count = len(refs) - 6 - 3 * N_BLOCKS
        found, (sampled, *raised) = refs[:count], refs[count : count + 1 + 2 * N_BLOCKS]
        *rows, keep, send, signal, losses, log_norm = refs[count + 1 + 2 * N_BLOCKS :]
        norms, picks = combine(found)
        log_norm[...] = norms
        losses[...] = norms - picks
        fill_signal(order, place, log_norm, sampled, raised[:N_BLOCKS], raised[N_BLOCKS:], signal)
    voc, width = keep.shape
    tile = min(C_TILE, width)

    @pl.loop(0, width // tile)
    def _(j):
        here = pl.ds(pl.multiple_of(j * tile, tile), tile)
        there = pl.ds(pl.multiple_of(part * width + j * tile, tile), tile)
        block = jnp.concatenate([r[:, there] for r in rows], axis=0)
        found = jnp.dot(signal[...], block, preferred_element_type=jnp.float32)
        keep[:, here] = found[:voc]
        send[:, here] = found[voc:].astype(jnp.bfloat16)


def gradient_part(part, order, place, rows, tables=(), sampled=None, raised=(), tops=(), signal=None):
    tokens, width = rows[0].shape
    count = N_BLOCKS * tokens
    both = signal.shape[0] if part else raised[0].shape[0]
    voc = both // 2
    out_shape = [
        jax.ShapeDtypeStruct((voc, width // PARTS), jnp.float32),
        jax.ShapeDtypeStruct((voc, width // PARTS), jnp.bfloat16),
    ]
    if part:
        inputs = (signal,)
    else:
        inputs = (*tables, sampled, *raised, *tops)
        out_shape += [
            jax.ShapeDtypeStruct((both, count), jnp.bfloat16),
            jax.ShapeDtypeStruct(sampled.shape, jnp.float32),
        ]
    return pl.pallas_call(
        functools.partial(gradient_kernel, part, order),
        in_specs=[scalars] + [whole] * (len(inputs) + len(rows)),
        out_specs=[whole] * len(out_shape),
        out_shape=out_shape,
        scratch_shapes=[] if part else [pltpu.VMEM(sampled.shape, jnp.float32)],
        compiler_params=pltpu.CompilerParams(vmem_limit_bytes=VMEM),
        cost_estimate=pl.CostEstimate(
            flops=2 * both * count * width // PARTS,
            bytes_accessed=2 * count * width // PARTS,
            transcendentals=0 if part else both * count,
        ),
    )(place, *inputs, *rows)


def tail_kernel(part, n_tokens, kept, got, momentum, hessian, *rest):
    *rest, fresh_buf, update_buf, loss_buf, sems = rest
    copies = []
    if n_tokens:
        losses, losses_other = rest[:2]
        *_, fresh_out, update_out, mean_loss = rest
        both = jnp.sum(losses[...] + losses_other[...], axis=(0, 1))
        loss_buf[...] = jnp.sum(both, axis=1, keepdims=True) / n_tokens
        copies.append(pltpu.make_async_copy(loss_buf, mean_loss, sems.at[0, 2]))
        copies[0].start()
    else:
        fresh_out, update_out = rest[-2:]
    width = kept.shape[1]
    tile = min(T_TILE, width)
    for j in range(width // tile):
        here = slice(j * tile, (j + 1) * tile)
        there = pl.ds(part * width + j * tile, tile)
        gradient = kept[:, here] + got[:, here].astype(jnp.float32)
        fresh = hess_decay * hessian[:, there].astype(jnp.float32) + (1.0 - hess_decay) * gradient * gradient
        scaled = momentum[:, there].astype(jnp.float32) * (1.0 / clip_scale)
        clipped = jnp.clip(scaled * pl.reciprocal(fresh, approx=False), -1.0, 1.0)
        fresh_buf[:, here] = fresh.astype(jnp.bfloat16)
        update_buf[:, here] = clipped.astype(jnp.bfloat16)
        for i, (buf, out) in enumerate(((fresh_buf, fresh_out), (update_buf, update_out))):
            copies.append(pltpu.make_async_copy(buf.at[:, here], out.at[:, there], sems.at[j, i]))
            copies[-1].start()
    for copy in copies:
        copy.wait()


def tail_part(part, kept, got, momentum, hessian, losses, n_tokens, earlier):
    voc, width = momentum.shape
    part_width = width // PARTS
    tile = min(T_TILE, part_width)
    out_specs = [anywhere] * 2
    out_shape = [jax.ShapeDtypeStruct((voc, width), jnp.bfloat16)] * 2
    last = part == PARTS - 1
    if last:
        out_specs.append(anywhere)
        out_shape.append(jax.ShapeDtypeStruct((1, 1), jnp.float32))
    else:
        losses = ()
    return pl.pallas_call(
        functools.partial(tail_kernel, part, n_tokens if last else 0),
        in_specs=[whole] * (4 + len(losses)) + [anywhere] * len(earlier),
        out_specs=out_specs,
        out_shape=out_shape,
        scratch_shapes=[pltpu.VMEM((voc, part_width), jnp.bfloat16)] * 2
        + [pltpu.VMEM((1, 1), jnp.float32), pltpu.SemaphoreType.DMA((part_width // tile, 3))],
        input_output_aliases={4 + len(losses) + i: i for i in range(len(earlier))},
        compiler_params=pltpu.CompilerParams(vmem_limit_bytes=VMEM),
        cost_estimate=pl.CostEstimate(
            flops=10 * voc * width // PARTS, bytes_accessed=14 * voc * width // PARTS, transcendentals=0
        ),
    )(kept, got, momentum, hessian, *losses, *earlier)


def gather_rounds(features):
    swap_x, swap_y = ([(i, i ^ m) for i in range(4)] for m in (1, 2))
    up = [(i, (i + 1) % N_BLOCKS) for i in range(N_BLOCKS)]
    down = [(j, i) for i, j in up]
    n = features.shape[0]
    size = n // LANES
    half = size // 2
    column = [features]
    for _ in range(1, N_BLOCKS):
        column.append(lax.ppermute(column[-1], "z", up))
    first = [lax.ppermute(features, "dp", swap) for swap in (swap_x, swap_y)]
    lanes = range(LANES)
    pieces = [[[(block, size, lane * size, 0, 0)] for lane in lanes] for block in column]
    for lane in lanes:
        pieces[0][lane] += [(array, size, lane * size, 1 + i, 0) for i, array in enumerate(first)]
    got = [[(array, lane * size) for array in first] for lane in lanes]
    after = []
    far, done = [], []
    for k in range(1, N_BLOCKS):
        last = k == N_BLOCKS - 1
        if last:
            after += done[:1]
        for lane in lanes:
            main = [(column[k], lane * size, size)]
            (from_x, x_at), (from_y, y_at) = got[lane]
            relayed = last and lane == LANES - 1
            if relayed:
                wanted = [main]
            else:
                wanted = [main + [(from_y, y_at, half)], main + [(from_x, x_at + half, half)]]
            if k == 2 and lane == LANES - 1:
                wanted.append(far)
            found = assemble(wanted, after)
            after = [found[0]]
            if k == 2 and lane == LANES - 1:
                above = lax.ppermute(found[2], "z", down)
            if relayed:
                (part,) = assemble([[(above, lane * size, size)]])
                pieces[k - 1][lane].append((lax.ppermute(part, "z", down), size, 0, 3, 0))
                found = found * 2
            sent = [lax.ppermute(f, "dp", swap) for f, swap in zip(found, (swap_x, swap_y))]
            for i, array in enumerate(sent):
                pieces[k][lane].append((array, size, 0, 1 + i, 0))
                if not relayed:
                    pieces[k - 1][lane].append((array, half, size, 3, i * half))
                if k == 1:
                    far.append((array, size, half))
            got[lane] = [(array, 0) for array in sent]
        if not last:
            done.append((yield [(k - 1, lane, pieces[k - 1][lane]) for lane in lanes]))
    for lane in lanes:
        pieces[-1][lane].append((above, size, lane * size, 3, 0))
        yield [(k, lane, pieces[k][lane]) for k in (N_BLOCKS - 2, N_BLOCKS - 1)]


def shards(features, head, momentum, hessian, true_labels, sampled_labels):
    n_dp, n_z = lax.axis_size("dp"), lax.axis_size("z")
    dp, z, core = lax.axis_index("dp"), lax.axis_index("z"), lax.axis_index("core")
    voc_dev = head.shape[0]
    n_rows = features.shape[0]
    swap_x = [(i, i ^ 1) for i in range(n_dp)]
    swap_y = [(i, i ^ 2) for i in range(n_dp)]
    swap_core = [(0, 1), (1, 0)]

    base = (dp * n_z + z) * 2
    ring = n_z == N_BLOCKS and n_dp == 4 and n_rows == 32 * LANES
    if ring:
        place, true, sampled = prepare(true_labels, sampled_labels, voc_dev)
    else:

        def in_order(labels):
            mine = labels.reshape(n_dp, N_BLOCKS, -1, 2, n_rows)[:, :, :, core]
            mine = mine.reshape(n_dp, N_BLOCKS, LANES, -1)
            return mine.transpose(1, 2, 0, 3).reshape(N_BLOCKS, LANES, 1, -1)

        true, sampled = in_order(true_labels), in_order(sampled_labels)
        owners = range(N_BLOCKS)
        place = jnp.stack(
            [dp, dp ^ 1, dp ^ 2, dp ^ 3, *owners, (base + core) * voc_dev, (base + 1 - core) * voc_dev]
        ).astype(jnp.int32)
    head_other = lax.ppermute(head, "core", swap_core)

    if ring:
        rounds = gather_rounds(features)
    else:
        column = jnp.split(lax.all_gather(features, "z", axis=0, tiled=True), N_BLOCKS, axis=0)
        n = column[0].shape[0]
        size = n // LANES
        column = [lax.all_gather(block, "dp", axis=0, tiled=True) for block in column]
        calls = [
            [
                (k, lane, [(block, size, d * n + lane * size, None, d * size) for d in range(n_dp)])
                for lane in range(LANES)
            ]
            for k, block in enumerate(column)
        ]
    blocks, order, stats, done = [], [], (), None
    for call in range(N_BLOCKS):
        groups = rounds.send(done) if ring else calls[call]
        order += [group[:2] for group in groups]
        *block, table, done = block_logits(place, true, groups, head, head_other, stats)
        blocks.append((*block, done))
        stats = (table,)

    rows, raised, tops = zip(*blocks)
    (stats,) = stats
    tables = from_all(combine_call(from_all(stats, "z", n_z)), "dp", n_dp)

    kept, summed = [], []
    signal = None
    for part in range(PARTS):
        if part:
            keep, send = gradient_part(part, order, place, rows, signal=signal)
        else:
            keep, send, signal, losses = gradient_part(part, order, place, rows, tables, sampled, raised, tops)
        kept.append(keep)
        summed.append(lax.ppermute(send, "core", swap_core))
    losses = (losses, lax.ppermute(losses, "core", swap_core))
    outs = ()
    for part in range(PARTS):
        outs = tail_part(
            part, kept[part], summed[part], momentum, hessian, losses, true_labels.shape[0], outs
        )
    fresh, clipped, mean_loss = outs
    return mean_loss[0, 0], fresh, clipped


def solution(mesh):
    n_dp, n_voc = mesh.shape["dp"], mesh.shape["vocab"]
    fine = Mesh(mesh.devices.reshape(n_dp, n_voc // 2, 2), ("dp", "z", "core"))
    rows = P(("dp", "z", "core"), None)
    return jax.shard_map(
        shards, mesh=fine, in_specs=(rows,) * 4 + (P(), P()), out_specs=(P(), rows, rows), check_vma=False
    )
```
